256 devices in a mesh: prefix: 32 (over y, z_lo, core), sample: 8 (over x, z_hi).
Axes of the slice: x: 4, y: 4, z: 8 (z_hi: 2, z_lo: 4; z = z_hi * 4 + z_lo), core: 2. Of those that a mesh axis runs over, the one named last changes fastest.
Arguments:
- queries: bfloat16 [256, 2, 8192], P(('prefix', 'sample')), may hold values from -100 to 100
- prefix_kv: bfloat16 [131072, 8, 256], P('prefix', 'sample'), may hold values from -8 to 8
- suffix_kv: bfloat16 [256, 1024, 8, 256], P(('prefix', 'sample')), may hold values from -10 to 10
- new_kv: bfloat16 [256, 2, 8, 256], P(('prefix', 'sample')), may hold values from -8 to 8
- lengths: int32 [256], P(('prefix', 'sample')), may hold values from 1 to 1024, 163840 in all
Outputs:
- attention: bfloat16 [256, 2, 8192], P(('prefix', 'sample'))
The draws below stay inside these ranges and needn't reach their ends.
Inputs may be any that keep to these rules, and one draw needn't show every extreme that they name: A sample's cache holds its entries in its first lengths slots; the others are not read.
All inputs are finite; a program needn't handle non-finite values. No bound on the sum of `lengths` on one device may be relied on, other than what follows from the above.
Results may differ from the reference program's by a relative error of at most 0.0024.
Values may be sent and summed in bfloat16 or wider, within the bound.
No kernel may reach another device: no remote copies, remote signals or barrier semaphores. Data moves between devices by JAX's collectives and lax.ppermute only.
A program may use at most 128 MiB of HBM per device.

```python
import math
import jax
import jax.numpy as jnp
import numpy as np
from jax import lax

HEADS = 64
KV_HEADS = 8
HEAD_DIM = 128
STEPS = 2
P_DEV = 4096
L_MAX = 1024
PREFIX = 131072
SAMPLES = 256
N_PREFIX = 32


def mixing_weights():
    topic_weight = math.sqrt(max(math.log(PREFIX / L_MAX) - 0.5, 1.0) / math.sqrt(HEAD_DIM))
    self_weight = (math.log(PREFIX) + 1.5) / math.sqrt(HEAD_DIM)
    return (topic_weight, self_weight)


def shared_parts(key):
    splits = jax.random.split(key, 2)
    topic = jax.random.truncated_normal(splits[0], -4.0, 4.0, (SAMPLES, KV_HEADS, HEAD_DIM), jnp.float32)
    fresh = jax.random.truncated_normal(splits[1], -4.0, 4.0, (SAMPLES, STEPS, KV_HEADS, HEAD_DIM), jnp.float32)
    return (topic, fresh)


def draw_queries(key, part):
    topic, fresh = shared_parts(key)
    key = jax.random.fold_in(key, 11)
    topic_weight, self_weight = mixing_weights()
    group_size = HEADS // KV_HEADS
    noise = jax.random.truncated_normal(key, -4.0, 4.0, (SAMPLES, STEPS, KV_HEADS, group_size, HEAD_DIM), jnp.float32)
    values = noise + topic_weight * topic[:, None, :, None, :] + self_weight * fresh[:, :, :, None, :]
    return values.reshape(SAMPLES, STEPS, HEADS * HEAD_DIM).astype(jnp.bfloat16)


def draw_prefix_kv(key, part):
    key = jax.random.fold_in(key, 12)
    first, second = jax.random.split(key)
    keys_part = jax.random.truncated_normal(first, -4.0, 4.0, (PREFIX, KV_HEADS, HEAD_DIM), jnp.float32)
    values_part = 2.0 * jax.random.truncated_normal(second, -4.0, 4.0, (PREFIX, KV_HEADS, HEAD_DIM), jnp.float32)
    return jnp.concatenate([keys_part, values_part], axis=-1).astype(jnp.bfloat16)


def draw_suffix_kv(key, part):
    topic, fresh = shared_parts(key)
    key = jax.random.fold_in(key, 13)
    first, second = jax.random.split(key)
    topic_weight, self_weight = mixing_weights()
    keys_part = jax.random.truncated_normal(first, -4.0, 4.0, (SAMPLES, L_MAX, KV_HEADS, HEAD_DIM), jnp.float32)
    keys_part = keys_part + topic_weight * topic[:, None, :, :]
    values_part = 2.0 * jax.random.truncated_normal(second, -4.0, 4.0, (SAMPLES, L_MAX, KV_HEADS, HEAD_DIM), jnp.float32)
    return jnp.concatenate([keys_part, values_part], axis=-1).astype(jnp.bfloat16)


def draw_new_kv(key, part):
    topic, fresh = shared_parts(key)
    key = jax.random.fold_in(key, 14)
    values_part = 2.0 * jax.random.truncated_normal(key, -4.0, 4.0, (SAMPLES, STEPS, KV_HEADS, HEAD_DIM), jnp.float32)
    return jnp.concatenate([fresh, values_part], axis=-1).astype(jnp.bfloat16)


def profile(amount, total, bound, skew):
    loads = [(1 << 20) // math.isqrt(standing ** skew) + 1 for standing in range(2, amount + 1)]
    spare, holding = total - bound - (amount - 1), [1] * (amount - 1)
    while spare > 0:
        free = [i for i in range(amount - 1) if holding[i] < bound]
        pool, remaining = sum([loads[i] for i in free]), spare
        for i in free:
            extra = min(bound - holding[i], max(1, remaining * loads[i] // pool), spare)
            holding[i] = holding[i] + extra
            spare = spare - extra
    return np.array([bound] + holding)


def uneven_parts(key, count, total, reach, skew):
    if count == 2:
        one = jax.random.randint(key, (), max(1, total - reach), min(reach, total - 1) + 1)
        return jnp.stack([one, total - one])
    tallies = jnp.asarray(profile(count, total, reach, skew), jnp.int32)
    couples = (count - 1) // 2
    donor, receiver = tallies[1:1 + 2 * couples:2], tallies[2:2 + 2 * couples:2]
    slack = jnp.minimum(donor - 1, reach - receiver)
    shifted = jax.random.randint(jax.random.fold_in(key, 1), (couples,), 0, 1 << 20) % (slack + 1)
    tallies = tallies.at[1:1 + 2 * couples:2].set(donor - shifted).at[2:2 + 2 * couples:2].set(receiver + shifted)
    return tallies[jax.random.permutation(jax.random.fold_in(key, 2), count)]


def setup_inputs(seed: int = 0) -> dict:
    keys = jax.random.split(jax.random.key(seed), 6)
    queries = draw_queries(jax.random.fold_in(keys[5], 71), 0)
    prefix_kv = draw_prefix_kv(jax.random.fold_in(keys[5], 71), 0)
    suffix_kv = draw_suffix_kv(jax.random.fold_in(keys[5], 71), 0)
    new_kv = draw_new_kv(jax.random.fold_in(keys[5], 71), 0)
    lengths = uneven_parts(keys[4], SAMPLES, SAMPLES * L_MAX * 5 // 8, L_MAX, 1).astype(jnp.int32)
    return {"queries": queries, "prefix_kv": prefix_kv, "suffix_kv": suffix_kv, "new_kv": new_kv, "lengths": lengths}


def prefix_head(paired):
    query_rows, head_kv = paired
    inverse_root = 1.0 / math.sqrt(HEAD_DIM)
    blocks = head_kv.reshape(N_PREFIX, P_DEV, 2 * HEAD_DIM)

    def absorb(carried, key_block):
        running_max, running_sum, numerator = carried
        scores = jnp.dot(query_rows, key_block[:, :HEAD_DIM].T, preferred_element_type=jnp.float32) * inverse_root
        block_peak = lax.optimization_barrier(jnp.max(scores, axis=1))
        weights = jnp.exp(scores - block_peak[:, None])
        block_total = lax.optimization_barrier(jnp.sum(weights, axis=1))
        block_numer = jnp.dot(weights.astype(jnp.bfloat16), key_block[:, HEAD_DIM:], preferred_element_type=jnp.float32)
        merged_max = jnp.maximum(running_max, block_peak)
        old_factor = jnp.exp(running_max - merged_max)
        new_factor = jnp.exp(block_peak - merged_max)
        return ((merged_max, running_sum * old_factor + block_total * new_factor, numerator * old_factor[:, None] + block_numer * new_factor[:, None]), None)
    row_count = query_rows.shape[0]
    initial = (jnp.full((row_count,), -1e+30, jnp.float32), jnp.zeros((row_count,), jnp.float32), jnp.zeros((row_count, HEAD_DIM), jnp.float32))
    outcome, unused = lax.scan(absorb, initial, blocks)
    return outcome

def sample_part(paired):
    query_one, suffix_one, new_one, length_one = paired
    group_size = HEADS // KV_HEADS
    inverse_root = 1.0 / math.sqrt(HEAD_DIM)
    query_heads = query_one.reshape(STEPS, KV_HEADS, group_size, HEAD_DIM).astype(jnp.float32)
    cached = jnp.concatenate([suffix_one, new_one], axis=0).astype(jnp.float32)
    scores = jnp.einsum('tkgd,lkd->tkgl', query_heads, cached[..., :HEAD_DIM]) * inverse_root
    positions = jnp.arange(L_MAX + STEPS)
    valid = jnp.where(positions[None, :] < L_MAX, positions[None, :] < length_one, (positions - L_MAX)[None, :] <= jnp.arange(STEPS)[:, None])
    masked = jnp.where(valid[:, None, None, :], scores, -1e+30)
    local_max = lax.optimization_barrier(jnp.max(masked, axis=-1))
    weights = jnp.exp(masked - local_max[..., None])
    local_total = lax.optimization_barrier(jnp.sum(weights, axis=-1))
    rounded = lax.optimization_barrier(weights.astype(jnp.bfloat16)).astype(jnp.float32)
    local_numer = jnp.einsum('tkgl,lkd->tkgd', rounded, cached[..., HEAD_DIM:])
    return (local_max, local_total, local_numer)

def reference(queries, prefix_kv, suffix_kv, new_kv, lengths):
    group_size = HEADS // KV_HEADS
    by_head = queries.reshape(SAMPLES, STEPS, KV_HEADS, group_size, HEAD_DIM).transpose(2, 0, 1, 3, 4)
    by_head = by_head.reshape(KV_HEADS, SAMPLES * STEPS * group_size, HEAD_DIM)
    block_max, block_total, block_numer = lax.map(prefix_head, (by_head, prefix_kv.transpose(1, 0, 2)))
    block_max = block_max.reshape(KV_HEADS, SAMPLES, STEPS, group_size).transpose(1, 2, 0, 3)
    block_total = block_total.reshape(KV_HEADS, SAMPLES, STEPS, group_size).transpose(1, 2, 0, 3)
    block_numer = block_numer.reshape(KV_HEADS, SAMPLES, STEPS, group_size, HEAD_DIM).transpose(1, 2, 0, 3, 4)
    local_max, local_total, local_numer = lax.map(sample_part, (queries, suffix_kv, new_kv, lengths))
    overall = jnp.maximum(block_max, local_max)
    prefix_factor = jnp.exp(block_max - overall)
    local_factor = jnp.exp(local_max - overall)
    numerator = block_numer * prefix_factor[..., None] + local_numer * local_factor[..., None]
    denominator = block_total * prefix_factor + local_total * local_factor
    attention = numerator / denominator[..., None]
    return attention.reshape(SAMPLES, STEPS, HEADS * HEAD_DIM).astype(jnp.bfloat16)
```

```python
import functools
import math

import jax
import jax.numpy as jnp
from jax import lax
from jax.experimental import pallas as pl
from jax.experimental.pallas import tpu as pltpu
from jax.sharding import Mesh, PartitionSpec as P

F32 = jnp.float32
BF16 = jnp.bfloat16
LANES = 128
Y, ZL, CORE, X, ZH = 4, 4, 2, 4, 2
AXES = ("y", "zl", "core", "x", "zh")
WIDE = ("zl", "x", "zh")
STEP = 32000.0
FRACTION = 32767.0
MASKED = -1e30
VMEM = pl.BlockSpec(memory_space=pltpu.VMEM)
SMEM = pl.BlockSpec(memory_space=pltpu.SMEM)


def params(mib):
    return pltpu.CompilerParams(vmem_limit_bytes=mib * 2**20)


def lane_select(shape, columns):
    lane = lax.broadcasted_iota(jnp.int32, shape, 1)
    out = jnp.zeros(shape, F32)
    for i, column in enumerate(columns):
        out = jnp.where(lane == i, column, out)
    return out


def code(values):
    peak = jnp.maximum(jnp.max(jnp.abs(values), axis=1, keepdims=True), 1e-30)
    power = jnp.ceil(jnp.log2(peak))
    coded = jnp.round(values * (jnp.exp2(-power) * STEP))
    return coded.astype(jnp.int32).astype(jnp.int16), power


def split_weight(weight):
    whole = jnp.floor(weight * 0.5)
    return whole, jnp.round((weight - 2.0 * whole) * (0.5 * FRACTION))


def join_weight(whole, part):
    return 2.0 * whole + part * (2.0 / FRACTION)


def spread_kernel(q_ref, out_ref, rows_ref, *, copies):
    steps = q_ref.shape[1]
    tiles = q_ref.shape[2] // LANES
    for c in range(tiles):
        rows_ref[steps * c : steps * (c + 1), :] = q_ref[0, :, LANES * c : LANES * (c + 1)].astype(F32)
    rows = rows_ref[...].astype(BF16)
    for i in range(copies):
        out_ref[i] = rows


def spread(queries):
    count = queries.shape[1] * queries.shape[2] // LANES
    return pl.pallas_call(
        functools.partial(spread_kernel, copies=ZL),
        out_shape=jax.ShapeDtypeStruct((ZL, count, LANES), BF16),
        in_specs=[VMEM],
        out_specs=VMEM,
        scratch_shapes=[pltpu.VMEM((count, LANES), F32)],
        compiler_params=params(16),
        name="spread",
    )(queries)


def local_kernel(len_ref, q_ref, kv_ref, new_ref, numer_ref, stat_ref, s_ref, new_pad, *, heads, chunk, factor):
    rows = q_ref.shape[1]
    group = rows // heads
    total = kv_ref.shape[0]
    news = new_ref.shape[0]
    q = q_ref[0]
    lane = lax.broadcasted_iota(jnp.int32, (rows, chunk), 1)
    row = lax.broadcasted_iota(jnp.int32, (rows, chunk), 0)
    own = (lane % heads) == (row // group)
    limit = jnp.where(own, lane, total)
    used = len_ref[0] * heads
    peak = None
    for j in range(total // chunk):
        s = lax.dot_general(
            q, kv_ref[j * chunk : (j + 1) * chunk, :LANES], (((1,), (1,)), ((), ())), preferred_element_type=F32
        )
        s = jnp.where(limit < used - j * chunk, s, MASKED)
        s_ref[:, j * chunk : (j + 1) * chunk] = s
        for i in range(chunk // LANES):
            part = s[:, i * LANES : (i + 1) * LANES]
            peak = part if peak is None else jnp.maximum(peak, part)
    new_pad[...] = jnp.zeros_like(new_pad)
    new_pad[:news, :] = new_ref[...]
    s_new = lax.dot_general(q, new_pad[:, :LANES], (((1,), (1,)), ((), ())), preferred_element_type=F32)
    steps = news // heads
    lane = lane[:, :LANES]
    row = row[:, :LANES]
    valid = own[:, :LANES] & (lane // heads <= row % steps)
    s_new = jnp.where(valid, s_new, MASKED)
    peak = jnp.max(jnp.maximum(peak, s_new), axis=1, keepdims=True)
    p_new = jnp.exp2((s_new - peak) * factor)
    weight = p_new
    numer = jnp.dot(p_new.astype(BF16), new_pad[:, LANES:], preferred_element_type=F32)
    for j in range(total // chunk):
        p = jnp.exp2((s_ref[:, j * chunk : (j + 1) * chunk] - peak) * factor)
        for i in range(chunk // LANES):
            weight = weight + p[:, i * LANES : (i + 1) * LANES]
        numer = numer + jnp.dot(
            p.astype(BF16), kv_ref[j * chunk : (j + 1) * chunk, LANES:], preferred_element_type=F32
        )
    numer_ref[...] = numer
    scale = factor / math.log2(math.e)
    stat_ref[...] = lane_select((rows, LANES), (peak * scale, jnp.sum(weight, axis=1, keepdims=True)))


def local(lengths, rows, cache, new, heads, factor):
    count = rows.shape[1]
    return pl.pallas_call(
        functools.partial(local_kernel, heads=heads, chunk=512, factor=factor),
        out_shape=(jax.ShapeDtypeStruct((count, LANES), F32), jax.ShapeDtypeStruct((count, LANES), F32)),
        in_specs=[SMEM, VMEM, VMEM, VMEM],
        out_specs=(VMEM, VMEM),
        scratch_shapes=[pltpu.VMEM((count, cache.shape[0]), F32), pltpu.VMEM((LANES, 2 * LANES), BF16)],
        compiler_params=params(32),
        name="local",
    )(lengths, rows, cache, new)


def document_kernel(q_ref, kv0_ref, kv1_ref, out_ref, s0_ref, s1_ref, *, tile, chunk, factor):
    rows = q_ref.shape[0]
    kv = (kv0_ref, kv1_ref)
    held = (s0_ref, s1_ref)
    pieces = kv0_ref.shape[0] // chunk
    units = [(r, b) for r in range(rows // tile) for b in range(2)]
    scale = factor / math.log2(math.e)

    def scores(u, j):
        r, b = units[u]
        s = lax.dot_general(
            q_ref[r * tile : (r + 1) * tile, :],
            kv[b][j * chunk : (j + 1) * chunk, :LANES],
            (((1,), (1,)), ((), ())),
            preferred_element_type=F32,
        )
        held[u % 2][:, j * chunk : (j + 1) * chunk] = s
        peak = s[:, :LANES]
        for i in range(1, chunk // LANES):
            peak = jnp.maximum(peak, s[:, i * LANES : (i + 1) * LANES])
        return peak

    running = None
    for j in range(pieces):
        part = scores(0, j)
        running = part if running is None else jnp.maximum(running, part)
    done = []
    stats = []
    for u, (r, b) in enumerate(units):
        peak = jnp.max(running, axis=1, keepdims=True)
        running = total = numer = None
        for j in range(pieces):
            if u + 1 < len(units):
                part = scores(u + 1, j)
                running = part if running is None else jnp.maximum(running, part)
            p = jnp.exp2((held[u % 2][:, j * chunk : (j + 1) * chunk] - peak) * factor)
            for i in range(chunk // LANES):
                part = p[:, i * LANES : (i + 1) * LANES]
                total = part if total is None else total + part
            part = jnp.dot(
                p.astype(BF16), kv[b][j * chunk : (j + 1) * chunk, LANES:], preferred_element_type=F32
            )
            numer = part if numer is None else numer + part
        done.append((peak, jnp.sum(total, axis=1, keepdims=True), numer))
        if b == 1:
            (peak0, total0, numer0), (peak1, total1, numer1) = done
            done = []
            top = jnp.maximum(peak0, peak1) * scale
            base = jnp.round(top * 2.0)
            factor0 = jnp.exp(peak0 * scale - base * 0.5)
            factor1 = jnp.exp(peak1 * scale - base * 0.5)
            coded, power = code(numer0 * factor0 + numer1 * factor1)
            out_ref[r * tile : (r + 1) * tile, :] = coded
            whole, part = split_weight(total0 * factor0 + total1 * factor1)
            for i in range(tile // LANES):
                at = slice(i * LANES, (i + 1) * LANES)
                stats.append((base[at], whole[at], part[at], power[at]))
    blocks = len(stats)
    columns = [stats[i][j] for j in range(4) for i in range(blocks)]
    across = jnp.transpose(lane_select((LANES, LANES), columns))
    out_ref[rows : rows + 16, :] = across[:16].astype(jnp.int32).astype(jnp.int16)


def document(rows, kv0, kv1, factor):
    count = rows.shape[0]
    tile = 256
    return pl.pallas_call(
        functools.partial(document_kernel, tile=tile, chunk=512, factor=factor),
        out_shape=jax.ShapeDtypeStruct((count + 16, LANES), jnp.int16),
        in_specs=[VMEM, VMEM, VMEM],
        out_specs=VMEM,
        scratch_shapes=[pltpu.VMEM((tile, kv0.shape[0]), F32)] * 2,
        compiler_params=params(40),
        name="document",
    )(rows, kv0, kv1)


def merge_kernel(*refs):
    parts, out_ref = refs[:-1], refs[-1]
    blocks = 4
    rows = parts[0].shape[0] - 16
    stats = [p[rows : rows + 16, :].astype(jnp.int32).astype(F32) for p in parts]
    tops = [s[0:blocks] for s in stats]
    top = functools.reduce(jnp.maximum, tops)
    shrink = [jnp.exp((t - top) * 0.5) for t in tops]
    weight = sum(
        f * join_weight(s[blocks : 2 * blocks], s[2 * blocks : 3 * blocks]) for f, s in zip(shrink, stats)
    )
    whole, part = split_weight(weight)
    scales = [f * (jnp.exp2(s[3 * blocks : 4 * blocks]) / STEP) for f, s in zip(shrink, stats)]
    used = blocks * (3 + len(parts))
    across = jnp.concatenate([top, whole, part] + scales + [jnp.zeros((LANES - used, LANES), F32)], axis=0)
    down = jnp.transpose(across)
    owners = LANES // 16
    for b in range(blocks):
        numer = None
        for i, p in enumerate(parts):
            at = 4 * (3 + i) + b
            term = p[b * LANES : (b + 1) * LANES, :].astype(jnp.int32).astype(F32) * down[:, at : at + 1]
            numer = term if numer is None else numer + term
        coded, power = code(numer)
        columns = [down[:, blocks * j + b : blocks * j + b + 1] for j in range(3)] + [power]
        tile = lane_select((LANES, LANES), columns).astype(jnp.int32).astype(jnp.int16)
        for s in range(owners):
            out_ref[b * owners + s, 0:16, :] = coded[16 * s : 16 * (s + 1), :]
            out_ref[b * owners + s, 16:32, :] = tile[16 * s : 16 * (s + 1), :]


def merge(parts):
    return pl.pallas_call(
        merge_kernel,
        out_shape=jax.ShapeDtypeStruct((32, 32, LANES), jnp.int16),
        in_specs=[VMEM] * len(parts),
        out_specs=VMEM,
        compiler_params=params(32),
        name="merge",
    )(*parts)


def finish_kernel(got_ref, numer_ref, stat_ref, out_ref, rows_ref, *, heads):
    steps = out_ref.shape[1]
    group = numer_ref.shape[0] // heads
    for k in range(heads):
        at = slice(k * group, (k + 1) * group)
        peak = stat_ref[at, 0:1]
        tiles = [got_ref[z * heads + k, 16:32, :].astype(jnp.int32).astype(F32) for z in range(ZL)]
        tops = [t[:, 0:1] * 0.5 for t in tiles]
        top = functools.reduce(jnp.maximum, tops, peak)
        shrink = jnp.exp(peak - top)
        numer = numer_ref[at, :] * shrink
        weight = stat_ref[at, 1:2] * shrink
        for z in range(ZL):
            shrink = jnp.exp(tops[z] - top)
            weight = weight + shrink * join_weight(tiles[z][:, 1:2], tiles[z][:, 2:3])
            coded = got_ref[z * heads + k, 0:16, :].astype(jnp.int32).astype(F32)
            numer = numer + coded * (shrink * (jnp.exp2(tiles[z][:, 3:4]) / STEP))
        rows_ref[at, :] = numer / weight
    for c in range(out_ref.shape[2] // LANES):
        out_ref[0, :, LANES * c : LANES * (c + 1)] = rows_ref[steps * c : steps * (c + 1), :].astype(BF16)


def finish(got, numer, stat, shape, heads):
    return pl.pallas_call(
        functools.partial(finish_kernel, heads=heads),
        out_shape=jax.ShapeDtypeStruct(shape, BF16),
        in_specs=[VMEM] * 3,
        out_specs=VMEM,
        scratch_shapes=[pltpu.VMEM(numer.shape, F32)],
        compiler_params=params(16),
        name="finish",
    )(got, numer, stat)


def per_device(queries, prefix_kv, suffix_kv, new_kv, lengths):
    positions, _, width = prefix_kv.shape
    head_dim = width // 2
    heads = suffix_kv.shape[2]
    factor = math.log2(math.e) / math.sqrt(head_dim)
    kv_own = prefix_kv.reshape(positions, width)
    kv_other = lax.ppermute(kv_own, "core", [(0, 1), (1, 0)])
    spread_rows = spread(queries)
    gathered = lax.all_to_all(
        spread_rows.reshape(ZL * heads, 16, LANES), WIDE, split_axis=0, concat_axis=0, tiled=True
    ).reshape(-1, LANES)
    cache = suffix_kv.reshape(-1, width)
    numer, stat = local(lengths, spread_rows, cache, new_kv.reshape(-1, width), heads, factor)
    others = [lax.ppermute(gathered, "y", [(j, (j - d) % Y) for j in range(Y)]) for d in (1, 3, 2)]
    parts = [document(gathered, kv_own, kv_other, factor)]
    for d, rows in zip((1, 3, 2), others):
        part = document(rows, kv_own, kv_other, factor)
        parts.append(lax.ppermute(part, "y", [(j, (j + d) % Y) for j in range(Y)]))
    merged = merge(parts)
    got = lax.all_to_all(merged, WIDE, split_axis=0, concat_axis=0, tiled=True)
    return finish(got, numer, stat, queries.shape, heads)


def solution(mesh):
    devices = mesh.devices.reshape(Y, ZL, CORE, X, ZH)
    fine = Mesh(devices, AXES)
    prefix, sample = ("y", "zl", "core"), ("x", "zh")
    owner = P(prefix + sample)
    in_specs = (owner, P(prefix, sample), owner, owner, owner)
    return jax.shard_map(per_device, mesh=fine, in_specs=in_specs, out_specs=owner, check_vma=False)
```

```python
import functools
import math

import jax
import jax.numpy as jnp
from jax import lax
from jax.experimental import pallas as pl
from jax.experimental.pallas import tpu as pltpu
from jax.sharding import Mesh, PartitionSpec as P

F32 = jnp.float32
BF16 = jnp.bfloat16
LANES = 128
Y, ZL, CORE, X, ZH = 4, 4, 2, 4, 2
AXES = ("y", "zl", "core", "x", "zh")
WIDE = ("zl", "x", "zh")
BITS = 14.9
FRACTION = 32767.0
MASKED = -1e30
VMEM = pl.BlockSpec(memory_space=pltpu.VMEM)
HBM = pl.BlockSpec(memory_space=pltpu.HBM)
SMEM = pl.BlockSpec(memory_space=pltpu.SMEM)


def params(mib):
    return pltpu.CompilerParams(vmem_limit_bytes=mib * 2**20)


def lane_select(shape, columns):
    lane = lax.broadcasted_iota(jnp.int32, shape, 1)
    out = jnp.zeros(shape, F32)
    for i, column in enumerate(columns):
        out = jnp.where(lane == i, column, out)
    return out


def toward_zero(values):
    return values.astype(jnp.int32).astype(F32)


def code(values):
    peak = jnp.maximum(jnp.max(jnp.abs(values), axis=1, keepdims=True), 1e-30)
    power = toward_zero(jnp.log2(peak) + 129.0) - 128.0
    coded = jnp.round(values * jnp.exp2(BITS - power))
    return coded.astype(jnp.int32).astype(jnp.int16), power


def split_weight(weight):
    whole = toward_zero(weight * 0.5)
    return whole, weight * (0.5 * FRACTION) - whole * FRACTION


def join_weight(whole, part):
    return 2.0 * whole + part * (2.0 / FRACTION)


def spread_kernel(q_ref, out_ref, held_ref, rows_ref, sem, *, copies):
    copy = pltpu.make_async_copy(q_ref, held_ref, sem)
    copy.start()
    copy.wait()
    steps = q_ref.shape[1]
    tiles = q_ref.shape[2] // LANES
    for c in range(tiles):
        rows_ref[steps * c : steps * (c + 1), :] = held_ref[0, :, LANES * c : LANES * (c + 1)].astype(F32)
    rows = rows_ref[...].astype(BF16)
    for i in range(copies):
        out_ref[i] = rows


def spread(queries):
    count = queries.shape[1] * queries.shape[2] // LANES
    return pl.pallas_call(
        functools.partial(spread_kernel, copies=ZL),
        out_shape=jax.ShapeDtypeStruct((ZL, count, LANES), BF16),
        in_specs=[HBM],
        out_specs=VMEM,
        scratch_shapes=[
            pltpu.VMEM(queries.shape, BF16),
            pltpu.VMEM((count, LANES), F32),
            pltpu.SemaphoreType.DMA(()),
        ],
        compiler_params=params(16),
        name="spread",
    )(pltpu.with_memory_space_constraint(queries, pltpu.HBM))


def local_kernel(
    len_ref, q_ref, cache_ref, new_ref, numer_ref, stat_ref, kv_ref, new_pad, s_ref, sems, *, heads, chunk, factor
):
    rows = q_ref.shape[1]
    group = rows // heads
    total = cache_ref.shape[0]
    news = new_ref.shape[0]
    new_pad[...] = jnp.zeros_like(new_pad)
    pieces = sems.shape[0] - 1
    size = total // pieces
    copies = [
        pltpu.make_async_copy(cache_ref.at[pl.ds(i * size, size)], kv_ref.at[pl.ds(i * size, size)], sems.at[i])
        for i in range(pieces)
    ]
    copies.append(pltpu.make_async_copy(new_ref, new_pad.at[pl.ds(0, news)], sems.at[pieces]))
    for copy in copies:
        copy.start()
    q = q_ref[0]
    lane = lax.broadcasted_iota(jnp.int32, (rows, chunk), 1)
    row = lax.broadcasted_iota(jnp.int32, (rows, chunk), 0)
    own = (lane % heads) == (row // group)
    limit = jnp.where(own, lane, total)
    used = len_ref[0] * heads
    peak = None
    for j in range(total // chunk):
        if j * chunk % size == 0:
            copies[j * chunk // size].wait()
        s = lax.dot_general(
            q, kv_ref[j * chunk : (j + 1) * chunk, :LANES], (((1,), (1,)), ((), ())), preferred_element_type=F32
        )
        s = jnp.where(limit < used - j * chunk, s, MASKED)
        s_ref[:, j * chunk : (j + 1) * chunk] = s
        for i in range(chunk // LANES):
            part = s[:, i * LANES : (i + 1) * LANES]
            peak = part if peak is None else jnp.maximum(peak, part)
    copies[pieces].wait()
    s_new = lax.dot_general(q, new_pad[:, :LANES], (((1,), (1,)), ((), ())), preferred_element_type=F32)
    steps = news // heads
    lane = lane[:, :LANES]
    row = row[:, :LANES]
    valid = own[:, :LANES] & (lane // heads <= row % steps)
    s_new = jnp.where(valid, s_new, MASKED)
    peak = jnp.max(jnp.maximum(peak, s_new), axis=1, keepdims=True)
    p_new = jnp.exp2((s_new - peak) * factor)
    weight = p_new
    numer = jnp.dot(p_new.astype(BF16), new_pad[:, LANES:], preferred_element_type=F32)
    for j in range(total // chunk):
        p = jnp.exp2((s_ref[:, j * chunk : (j + 1) * chunk] - peak) * factor)
        for i in range(chunk // LANES):
            weight = weight + p[:, i * LANES : (i + 1) * LANES]
        numer = numer + jnp.dot(
            p.astype(BF16), kv_ref[j * chunk : (j + 1) * chunk, LANES:], preferred_element_type=F32
        )
    numer_ref[...] = numer
    scale = factor / math.log2(math.e)
    stat_ref[...] = lane_select((rows, LANES), (peak * scale, jnp.sum(weight, axis=1, keepdims=True)))


def local(lengths, rows, cache, new, heads, factor):
    count = rows.shape[1]
    pieces = 8
    return pl.pallas_call(
        functools.partial(local_kernel, heads=heads, chunk=512, factor=factor),
        out_shape=(jax.ShapeDtypeStruct((count, LANES), F32), jax.ShapeDtypeStruct((count, LANES), F32)),
        in_specs=[SMEM, VMEM, HBM, HBM],
        out_specs=(VMEM, VMEM),
        scratch_shapes=[
            pltpu.VMEM(cache.shape, BF16),
            pltpu.VMEM((LANES, 2 * LANES), BF16),
            pltpu.VMEM((count, cache.shape[0]), F32),
            pltpu.SemaphoreType.DMA((pieces + 1,)),
        ],
        compiler_params=params(24),
        name="local",
    )(lengths, rows, *(pltpu.with_memory_space_constraint(a, pltpu.HBM) for a in (cache, new)))


def document_kernel(*refs, groups, fetch, tile, chunk, factor):
    q_refs, kv = refs[:groups], list(refs[groups : groups + 2])
    out_refs = refs[groups + 2 : 2 * groups + 2]
    held = refs[2 * groups + 2 : 2 * groups + 4]
    rows = q_refs[0].shape[0]
    positions = kv[0].shape[0]
    copies = []
    if fetch:
        far_ref, (kv[1], sems) = kv[1], refs[2 * groups + 4 :]
        size = positions // sems.shape[0]
        for i in range(sems.shape[0]):
            at = pl.ds(i * size, size)
            copies.append(pltpu.make_async_copy(far_ref.at[at], kv[1].at[at], sems.at[i]))
            copies[i].start()
    pieces = positions // chunk
    tiles = rows // tile
    units = [(g, b, r) for g in range(groups) for b in range(2) for r in range(tiles)]
    scale = factor / math.log2(math.e)

    def scores(u, j):
        g, b, r = units[u]
        if u == tiles and j == 0:
            for copy in copies:
                copy.wait()
        s = lax.dot_general(
            q_refs[g][r * tile : (r + 1) * tile, :],
            kv[b][j * chunk : (j + 1) * chunk, :LANES],
            (((1,), (1,)), ((), ())),
            preferred_element_type=F32,
        )
        held[u % 2][:, j * chunk : (j + 1) * chunk] = s
        peak = s[:, :LANES]
        for i in range(1, chunk // LANES):
            peak = jnp.maximum(peak, s[:, i * LANES : (i + 1) * LANES])
        return peak

    running = None
    for j in range(pieces):
        part = scores(0, j)
        running = part if running is None else jnp.maximum(running, part)
    done = {}
    stats = []
    for u, (g, b, r) in enumerate(units):
        peak = jnp.max(running, axis=1, keepdims=True)
        running = total = numer = None
        for j in range(pieces):
            if u + 1 < len(units):
                part = scores(u + 1, j)
                running = part if running is None else jnp.maximum(running, part)
            p = jnp.exp2((held[u % 2][:, j * chunk : (j + 1) * chunk] - peak) * factor)
            for i in range(chunk // LANES):
                part = p[:, i * LANES : (i + 1) * LANES]
                total = part if total is None else total + part
            part = jnp.dot(
                p.astype(BF16), kv[b][j * chunk : (j + 1) * chunk, LANES:], preferred_element_type=F32
            )
            numer = part if numer is None else numer + part
        done[b, r] = (peak, jnp.sum(total, axis=1, keepdims=True), numer)
        if b == 1:
            (peak0, total0, numer0), (peak1, total1, numer1) = done[0, r], done[1, r]
            base = toward_zero(jnp.maximum(peak0, peak1) * (2.0 * scale))
            ground = base * (0.5 / scale)
            factor0 = jnp.exp2((peak0 - ground) * factor)
            factor1 = jnp.exp2((peak1 - ground) * factor)
            coded, power = code(numer0 * factor0 + numer1 * factor1)
            out_refs[g][r * tile : (r + 1) * tile, :] = coded
            weight = total0 * factor0 + total1 * factor1
            for i in range(tile // LANES):
                at = slice(i * LANES, (i + 1) * LANES)
                stats.append((base[at], weight[at], weight[at], power[at]))
            if len(stats) * LANES == rows:
                side = lane_select((LANES, LANES), [stat[j] for j in range(4) for stat in stats])
                whole, part = split_weight(side)
                lane = lax.broadcasted_iota(jnp.int32, (LANES, LANES), 1) // len(stats)
                side = jnp.where(lane == 1, whole, jnp.where(lane == 2, part, side))
                out_refs[g][rows : rows + LANES, :] = side.astype(jnp.int32).astype(jnp.int16)
                stats = []


def document(groups, kv0, kv1, factor, fetch=False):
    count = groups[0].shape[0]
    tile = 256
    out = jax.ShapeDtypeStruct((count + LANES, LANES), jnp.int16)
    scratch = [pltpu.VMEM((tile, kv0.shape[0]), F32)] * 2
    if fetch:
        kv1 = pltpu.with_memory_space_constraint(kv1, pltpu.HBM)
        scratch += [pltpu.VMEM(kv1.shape, BF16), pltpu.SemaphoreType.DMA((2,))]
    return pl.pallas_call(
        functools.partial(
            document_kernel, groups=len(groups), fetch=fetch, tile=tile, chunk=512, factor=factor
        ),
        out_shape=[out] * len(groups),
        in_specs=[VMEM] * (len(groups) + 1) + [HBM if fetch else VMEM],
        out_specs=[VMEM] * len(groups),
        scratch_shapes=scratch,
        compiler_params=params(40),
        name="document",
    )(*groups, kv0, kv1)


def merge_kernel(*refs):
    parts, out_ref = refs[:-1], refs[-1]
    blocks = 4
    owners = LANES // 16
    rows = parts[0].shape[0] - LANES
    lane = lax.broadcasted_iota(jnp.int32, (LANES, LANES), 1)

    def shifted(values, lanes):
        return pltpu.roll(values, lanes % LANES, 1)

    stats = [p[rows : rows + LANES, :].astype(jnp.int32).astype(F32) for p in parts]
    top = functools.reduce(jnp.maximum, stats)
    shrink = [jnp.exp(jnp.minimum(s - top, 0.0) * 0.5) for s in stats]
    weight = sum(f * join_weight(shifted(s, -blocks), shifted(s, -2 * blocks)) for f, s in zip(shrink, stats))
    whole, part = split_weight(weight)
    scales = [f * jnp.exp2(shifted(s, -3 * blocks) - BITS) for f, s in zip(shrink, stats)]
    side = jnp.where(lane < blocks, top, jnp.where(lane < 2 * blocks, shifted(whole, blocks), shifted(part, 2 * blocks)))
    for b in range(blocks):
        numer = None
        for p, scale in zip(parts, scales):
            term = p[b * LANES : (b + 1) * LANES, :].astype(jnp.int32).astype(F32) * scale[:, b : b + 1]
            numer = term if numer is None else numer + term
        coded, power = code(numer)
        tile = side if b == 0 else shifted(side, -b)
        tile = jnp.where(lane < 3 * blocks, tile, power).astype(jnp.int32).astype(jnp.int16)
        for s in range(owners):
            out_ref[b * owners + s, 0:16, :] = coded[16 * s : 16 * (s + 1), :]
            out_ref[b * owners + s, 16:32, :] = tile[16 * s : 16 * (s + 1), :]


def merge(parts):
    return pl.pallas_call(
        merge_kernel,
        out_shape=jax.ShapeDtypeStruct((32, 32, LANES), jnp.int16),
        in_specs=[VMEM] * len(parts),
        out_specs=VMEM,
        compiler_params=params(32),
        name="merge",
    )(*parts)


def finish_kernel(got_ref, numer_ref, stat_ref, out_ref, rows_ref, *, heads):
    steps = out_ref.shape[1]
    rows = numer_ref.shape[0]

    def read(z, first):
        part = got_ref[z * heads : (z + 1) * heads, first : first + 16, :]
        return part.astype(jnp.int32).astype(F32).reshape(rows, LANES)

    tiles = [read(z, 16) for z in range(ZL)]
    peak = stat_ref[:, 0:1]
    tops = [t[:, 0:1] * 0.5 for t in tiles]
    top = functools.reduce(jnp.maximum, tops, peak)
    shrink = jnp.exp(peak - top)
    numer = numer_ref[...] * shrink
    weight = stat_ref[:, 1:2] * shrink
    for z, t in enumerate(tiles):
        shrink = jnp.exp(tops[z] - top)
        weight = weight + shrink * join_weight(t[:, 4:5], t[:, 8:9])
        numer = numer + read(z, 0) * (shrink * jnp.exp2(t[:, 12:13] - BITS))
    rows_ref[...] = numer / weight
    for c in range(out_ref.shape[2] // LANES):
        out_ref[0, :, LANES * c : LANES * (c + 1)] = rows_ref[steps * c : steps * (c + 1), :].astype(BF16)


def finish(got, numer, stat, shape, heads):
    return pl.pallas_call(
        functools.partial(finish_kernel, heads=heads),
        out_shape=jax.ShapeDtypeStruct(shape, BF16),
        in_specs=[VMEM] * 3,
        out_specs=VMEM,
        scratch_shapes=[pltpu.VMEM(numer.shape, F32)],
        compiler_params=params(16),
        name="finish",
    )(got, numer, stat)


def per_device(queries, prefix_kv, suffix_kv, new_kv, lengths):
    positions, _, width = prefix_kv.shape
    head_dim = width // 2
    heads = suffix_kv.shape[2]
    factor = math.log2(math.e) / math.sqrt(head_dim)
    kv_own = prefix_kv.reshape(positions, width)
    kv_other = lax.ppermute(kv_own, "core", [(0, 1), (1, 0)])
    spread_rows = spread(queries)
    gathered = lax.all_to_all(
        spread_rows.reshape(ZL * heads, 16, LANES), WIDE, split_axis=0, concat_axis=0, tiled=True
    ).reshape(-1, LANES)
    others = [lax.ppermute(gathered, "y", [(j, (j - d) % Y) for j in range(Y)]) for d in (1, 3, 2)]
    parts = document(others[:1], kv_other, kv_own, factor, fetch=True)
    parts, others = lax.optimization_barrier((parts, others))
    parts += document(others[1:], kv_own, kv_other, factor)
    parts = [lax.ppermute(p, "y", [(j, (j + d) % Y) for j in range(Y)]) for d, p in zip((1, 3, 2), parts)]
    parts += document([gathered], kv_own, kv_other, factor)
    merged = merge(parts)
    merged, spread_rows = lax.optimization_barrier((merged, spread_rows))
    got = lax.all_to_all(merged, WIDE, split_axis=0, concat_axis=0, tiled=True)
    cache = suffix_kv.reshape(-1, width)
    numer, stat = local(lengths, spread_rows, cache, new_kv.reshape(-1, width), heads, factor)
    return finish(got, numer, stat, queries.shape, heads)


def solution(mesh):
    devices = mesh.devices.reshape(Y, ZL, CORE, X, ZH)
    fine = Mesh(devices, AXES)
    prefix, sample = ("y", "zl", "core"), ("x", "zh")
    owner = P(prefix + sample)
    in_specs = (owner, P(prefix, sample), owner, owner, owner)
    return jax.shard_map(per_device, mesh=fine, in_specs=in_specs, out_specs=owner, check_vma=False)
```

```python
import functools
import math

import jax
import jax.numpy as jnp
from jax import lax
from jax.experimental import pallas as pl
from jax.experimental.pallas import tpu as pltpu
from jax.sharding import Mesh, PartitionSpec as P

F32 = jnp.float32
BF16 = jnp.bfloat16
LANES = 128
YH, YL, ZL, CORE, X, ZH = 2, 2, 4, 2, 4, 2
AXES = ("yh", "yl", "zl", "core", "x", "zh")
WIDE = ("zl", "x", "zh")
SWAP = [(0, 1), (1, 0)]
BITS = 14.9
FRACTION = 32767.0
MASKED = -1e30
VMEM = pl.BlockSpec(memory_space=pltpu.VMEM)
HBM = pl.BlockSpec(memory_space=pltpu.HBM)
SMEM = pl.BlockSpec(memory_space=pltpu.SMEM)


def params(mib):
    return pltpu.CompilerParams(vmem_limit_bytes=mib * 2**20)


def lane_select(shape, columns):
    lane = lax.broadcasted_iota(jnp.int32, shape, 1)
    out = jnp.zeros(shape, F32)
    for i, column in enumerate(columns):
        out = jnp.where(lane == i, column, out)
    return out


def toward_zero(values):
    return values.astype(jnp.int32).astype(F32)


def code(values):
    peak = jnp.maximum(jnp.max(jnp.abs(values), axis=1, keepdims=True), 1e-30)
    power = toward_zero(jnp.log2(peak) + 129.0) - 128.0
    coded = jnp.round(values * jnp.exp2(BITS - power))
    return coded.astype(jnp.int32).astype(jnp.int16), power


def split_weight(weight):
    whole = toward_zero(weight * 0.5)
    return whole, weight * (0.5 * FRACTION) - whole * FRACTION


def join_weight(whole, part):
    return 2.0 * whole + part * (2.0 / FRACTION)


def spread_kernel(q_ref, out_ref, held_ref, rows_ref, sem, *, copies):
    copy = pltpu.make_async_copy(q_ref, held_ref, sem)
    copy.start()
    copy.wait()
    steps = q_ref.shape[1]
    tiles = q_ref.shape[2] // LANES
    for c in range(tiles):
        rows_ref[steps * c : steps * (c + 1), :] = held_ref[0, :, LANES * c : LANES * (c + 1)].astype(F32)
    rows = rows_ref[...].astype(BF16)
    for i in range(copies):
        out_ref[i] = rows


def spread(queries):
    count = queries.shape[1] * queries.shape[2] // LANES
    return pl.pallas_call(
        functools.partial(spread_kernel, copies=YL * ZL),
        out_shape=jax.ShapeDtypeStruct((YL * ZL, count, LANES), BF16),
        in_specs=[HBM],
        out_specs=VMEM,
        scratch_shapes=[
            pltpu.VMEM(queries.shape, BF16),
            pltpu.VMEM((count, LANES), F32),
            pltpu.SemaphoreType.DMA(()),
        ],
        compiler_params=params(16),
        name="spread",
    )(pltpu.with_memory_space_constraint(queries, pltpu.HBM))


def local_kernel(
    len_ref, q_ref, cache_ref, new_ref, numer_ref, stat_ref, kv_ref, new_pad, s_ref, sems, *, heads, chunk, factor
):
    rows = q_ref.shape[1]
    group = rows // heads
    total = cache_ref.shape[0]
    news = new_ref.shape[0]
    new_pad[...] = jnp.zeros_like(new_pad)
    pieces = sems.shape[0] - 1
    size = total // pieces
    copies = [
        pltpu.make_async_copy(cache_ref.at[pl.ds(i * size, size)], kv_ref.at[pl.ds(i * size, size)], sems.at[i])
        for i in range(pieces)
    ]
    copies.append(pltpu.make_async_copy(new_ref, new_pad.at[pl.ds(0, news)], sems.at[pieces]))
    for copy in copies:
        copy.start()
    q = q_ref[0]
    lane = lax.broadcasted_iota(jnp.int32, (rows, chunk), 1)
    row = lax.broadcasted_iota(jnp.int32, (rows, chunk), 0)
    own = (lane % heads) == (row // group)
    limit = jnp.where(own, lane, total)
    used = len_ref[0] * heads
    peak = None
    for j in range(total // chunk):
        if j * chunk % size == 0:
            copies[j * chunk // size].wait()
        s = lax.dot_general(
            q, kv_ref[j * chunk : (j + 1) * chunk, :LANES], (((1,), (1,)), ((), ())), preferred_element_type=F32
        )
        s = jnp.where(limit < used - j * chunk, s, MASKED)
        s_ref[:, j * chunk : (j + 1) * chunk] = s
        for i in range(chunk // LANES):
            part = s[:, i * LANES : (i + 1) * LANES]
            peak = part if peak is None else jnp.maximum(peak, part)
    copies[pieces].wait()
    s_new = lax.dot_general(q, new_pad[:, :LANES], (((1,), (1,)), ((), ())), preferred_element_type=F32)
    steps = news // heads
    lane = lane[:, :LANES]
    row = row[:, :LANES]
    valid = own[:, :LANES] & (lane // heads <= row % steps)
    s_new = jnp.where(valid, s_new, MASKED)
    peak = jnp.max(jnp.maximum(peak, s_new), axis=1, keepdims=True)
    p_new = jnp.exp2((s_new - peak) * factor)
    weight = p_new
    numer = jnp.dot(p_new.astype(BF16), new_pad[:, LANES:], preferred_element_type=F32)
    for j in range(total // chunk):
        p = jnp.exp2((s_ref[:, j * chunk : (j + 1) * chunk] - peak) * factor)
        for i in range(chunk // LANES):
            weight = weight + p[:, i * LANES : (i + 1) * LANES]
        numer = numer + jnp.dot(
            p.astype(BF16), kv_ref[j * chunk : (j + 1) * chunk, LANES:], preferred_element_type=F32
        )
    numer_ref[...] = numer
    scale = factor / math.log2(math.e)
    stat_ref[...] = lane_select((rows, LANES), (peak * scale, jnp.sum(weight, axis=1, keepdims=True)))


def local(lengths, rows, cache, new, heads, factor):
    count = rows.shape[1]
    pieces = 8
    return pl.pallas_call(
        functools.partial(local_kernel, heads=heads, chunk=512, factor=factor),
        out_shape=(jax.ShapeDtypeStruct((count, LANES), F32), jax.ShapeDtypeStruct((count, LANES), F32)),
        in_specs=[SMEM, VMEM, HBM, HBM],
        out_specs=(VMEM, VMEM),
        scratch_shapes=[
            pltpu.VMEM(cache.shape, BF16),
            pltpu.VMEM((LANES, 2 * LANES), BF16),
            pltpu.VMEM((count, cache.shape[0]), F32),
            pltpu.SemaphoreType.DMA((pieces + 1,)),
        ],
        compiler_params=params(24),
        name="local",
    )(lengths, rows, *(pltpu.with_memory_space_constraint(a, pltpu.HBM) for a in (cache, new)))


def document_kernel(low_ref, q_ref, *refs, picks, fetch, tile, chunk, factor):
    groups = len(picks)
    kv = list(refs[:2])
    out_refs = refs[2 : groups + 2]
    held = refs[groups + 2 : groups + 4]
    rows = q_ref.shape[1]
    low = low_ref[0]
    blocks_of = [1 - low if pick else low for pick in picks]
    positions = kv[0].shape[0]
    copies = []
    if fetch:
        far_ref, (kv[1], sems) = kv[1], refs[groups + 4 :]
        size = positions // sems.shape[0]
        for i in range(sems.shape[0]):
            at = pl.ds(i * size, size)
            copies.append(pltpu.make_async_copy(far_ref.at[at], kv[1].at[at], sems.at[i]))
            copies[i].start()
    pieces = positions // chunk
    tiles = rows // tile
    units = [(g, b, r) for g in range(groups) for b in range(2) for r in range(tiles)]
    scale = factor / math.log2(math.e)

    def scores(u, j):
        g, b, r = units[u]
        if u == tiles and j == 0:
            for copy in copies:
                copy.wait()
        s = lax.dot_general(
            q_ref[blocks_of[g], r * tile : (r + 1) * tile, :],
            kv[b][j * chunk : (j + 1) * chunk, :LANES],
            (((1,), (1,)), ((), ())),
            preferred_element_type=F32,
        )
        held[u % 2][:, j * chunk : (j + 1) * chunk] = s
        peak = s[:, :LANES]
        for i in range(1, chunk // LANES):
            peak = jnp.maximum(peak, s[:, i * LANES : (i + 1) * LANES])
        return peak

    running = None
    for j in range(pieces):
        part = scores(0, j)
        running = part if running is None else jnp.maximum(running, part)
    done = {}
    stats = []
    for u, (g, b, r) in enumerate(units):
        peak = jnp.max(running, axis=1, keepdims=True)
        running = total = numer = None
        for j in range(pieces):
            if u + 1 < len(units):
                part = scores(u + 1, j)
                running = part if running is None else jnp.maximum(running, part)
            p = jnp.exp2((held[u % 2][:, j * chunk : (j + 1) * chunk] - peak) * factor)
            for i in range(chunk // LANES):
                part = p[:, i * LANES : (i + 1) * LANES]
                total = part if total is None else total + part
            part = jnp.dot(
                p.astype(BF16), kv[b][j * chunk : (j + 1) * chunk, LANES:], preferred_element_type=F32
            )
            numer = part if numer is None else numer + part
        done[b, r] = (peak, jnp.sum(total, axis=1, keepdims=True), numer)
        if b == 1:
            (peak0, total0, numer0), (peak1, total1, numer1) = done[0, r], done[1, r]
            base = toward_zero(jnp.maximum(peak0, peak1) * (2.0 * scale))
            ground = base * (0.5 / scale)
            factor0 = jnp.exp2((peak0 - ground) * factor)
            factor1 = jnp.exp2((peak1 - ground) * factor)
            coded, power = code(numer0 * factor0 + numer1 * factor1)
            out_refs[g][r * tile : (r + 1) * tile, :] = coded
            weight = total0 * factor0 + total1 * factor1
            for i in range(tile // LANES):
                at = slice(i * LANES, (i + 1) * LANES)
                stats.append((base[at], weight[at], weight[at], power[at]))
            if len(stats) * LANES == rows:
                side = lane_select((LANES, LANES), [stat[j] for j in range(4) for stat in stats])
                whole, part = split_weight(side)
                lane = lax.broadcasted_iota(jnp.int32, (LANES, LANES), 1) // len(stats)
                side = jnp.where(lane == 1, whole, jnp.where(lane == 2, part, side))
                out_refs[g][rows : rows + LANES, :] = side.astype(jnp.int32).astype(jnp.int16)
                stats = []


def document(low, pair, picks, kv0, kv1, factor, fetch=False):
    tile = 256
    out = jax.ShapeDtypeStruct((pair.shape[1] + LANES, LANES), jnp.int16)
    scratch = [pltpu.VMEM((tile, kv0.shape[0]), F32)] * 2
    if fetch:
        kv1 = pltpu.with_memory_space_constraint(kv1, pltpu.HBM)
        scratch += [pltpu.VMEM(kv1.shape, BF16), pltpu.SemaphoreType.DMA((2,))]
    return pl.pallas_call(
        functools.partial(document_kernel, picks=picks, fetch=fetch, tile=tile, chunk=512, factor=factor),
        out_shape=[out] * len(picks),
        in_specs=[SMEM, VMEM, VMEM, HBM if fetch else VMEM],
        out_specs=[VMEM] * len(picks),
        scratch_shapes=scratch,
        compiler_params=params(40),
        name="document",
    )(low, pair, kv0, kv1)


def merge_kernel(*refs):
    parts, out_ref = refs[:-1], refs[-1]
    blocks = 4
    owners = LANES // 16
    rows = parts[0].shape[0] - LANES
    lane = lax.broadcasted_iota(jnp.int32, (LANES, LANES), 1)

    def shifted(values, lanes):
        return pltpu.roll(values, lanes % LANES, 1)

    stats = [p[rows : rows + LANES, :].astype(jnp.int32).astype(F32) for p in parts]
    top = functools.reduce(jnp.maximum, stats)
    shrink = [jnp.exp(jnp.minimum(s - top, 0.0) * 0.5) for s in stats]
    weight = sum(f * join_weight(shifted(s, -blocks), shifted(s, -2 * blocks)) for f, s in zip(shrink, stats))
    whole, part = split_weight(weight)
    scales = [f * jnp.exp2(shifted(s, -3 * blocks) - BITS) for f, s in zip(shrink, stats)]
    side = jnp.where(lane < blocks, top, jnp.where(lane < 2 * blocks, shifted(whole, blocks), shifted(part, 2 * blocks)))
    for b in range(blocks):
        numer = None
        for p, scale in zip(parts, scales):
            term = p[b * LANES : (b + 1) * LANES, :].astype(jnp.int32).astype(F32) * scale[:, b : b + 1]
            numer = term if numer is None else numer + term
        coded, power = code(numer)
        tile = side if b == 0 else shifted(side, -b)
        tile = jnp.where(lane < 3 * blocks, tile, power).astype(jnp.int32).astype(jnp.int16)
        for s in range(owners):
            out_ref[b * owners + s, 0:16, :] = coded[16 * s : 16 * (s + 1), :]
            out_ref[b * owners + s, 16:32, :] = tile[16 * s : 16 * (s + 1), :]


def merge(parts):
    return pl.pallas_call(
        merge_kernel,
        out_shape=jax.ShapeDtypeStruct((32, 32, LANES), jnp.int16),
        in_specs=[VMEM] * len(parts),
        out_specs=VMEM,
        compiler_params=params(32),
        name="merge",
    )(*parts)


def finish_kernel(got_ref, numer_ref, stat_ref, out_ref, rows_ref, *, heads):
    steps = out_ref.shape[1]
    rows = numer_ref.shape[0]

    def read(z, first):
        part = got_ref[z * heads : (z + 1) * heads, first : first + 16, :]
        return part.astype(jnp.int32).astype(F32).reshape(rows, LANES)

    tiles = [read(z, 16) for z in range(ZL)]
    peak = stat_ref[:, 0:1]
    tops = [t[:, 0:1] * 0.5 for t in tiles]
    top = functools.reduce(jnp.maximum, tops, peak)
    shrink = jnp.exp(peak - top)
    numer = numer_ref[...] * shrink
    weight = stat_ref[:, 1:2] * shrink
    for z, t in enumerate(tiles):
        shrink = jnp.exp(tops[z] - top)
        weight = weight + shrink * join_weight(t[:, 4:5], t[:, 8:9])
        numer = numer + read(z, 0) * (shrink * jnp.exp2(t[:, 12:13] - BITS))
    rows_ref[...] = numer / weight
    for c in range(out_ref.shape[2] // LANES):
        out_ref[0, :, LANES * c : LANES * (c + 1)] = rows_ref[steps * c : steps * (c + 1), :].astype(BF16)


def finish(got, numer, stat, shape, heads):
    return pl.pallas_call(
        functools.partial(finish_kernel, heads=heads),
        out_shape=jax.ShapeDtypeStruct(shape, BF16),
        in_specs=[VMEM] * 3,
        out_specs=VMEM,
        scratch_shapes=[pltpu.VMEM(numer.shape, F32)],
        compiler_params=params(16),
        name="finish",
    )(got, numer, stat)


def per_device(queries, prefix_kv, suffix_kv, new_kv, lengths):
    positions, _, width = prefix_kv.shape
    head_dim = width // 2
    heads = suffix_kv.shape[2]
    factor = math.log2(math.e) / math.sqrt(head_dim)
    kv_own = prefix_kv.reshape(positions, width)
    kv_other = lax.ppermute(kv_own, "core", SWAP)
    low = lax.axis_index("yl").astype(jnp.int32).reshape(1)

    def after(array, *earlier):
        return lax.optimization_barrier((array, earlier))[0]

    def across(array):
        return lax.ppermute(array, "yh", SWAP)

    def diagonal(array):
        return lax.ppermute(array, ("yh", "yl"), [(j, YH * YL - 1 - j) for j in range(YH * YL)])

    spread_rows = spread(queries)
    count = spread_rows.shape[0] * heads
    pair = lax.all_to_all(
        spread_rows.reshape(count, -1, LANES), ("yl",) + WIDE, split_axis=0, concat_axis=0, tiled=True
    ).reshape(YL, -1, LANES)
    far = diagonal(pair)
    near_part = document(low, pair, (1,), kv_other, kv_own, factor, fetch=True)
    near_part, far = lax.optimization_barrier((near_part, far))
    far_parts = document(low, far, (1, 0), kv_own, kv_other, factor)
    own_part = document(low, after(pair, far_parts), (0,), kv_own, kv_other, factor)
    parts = [
        own_part[0],
        lax.ppermute(near_part[0], "yl", SWAP),
        diagonal(far_parts[0]),
        across(far_parts[1]),
    ]
    merged = merge(parts)
    merged, spread_rows = lax.optimization_barrier((merged, spread_rows))
    got = lax.all_to_all(merged, WIDE, split_axis=0, concat_axis=0, tiled=True)
    cache = suffix_kv.reshape(-1, width)
    numer, stat = local(lengths, spread_rows, cache, new_kv.reshape(-1, width), heads, factor)
    return finish(got, numer, stat, queries.shape, heads)


def solution(mesh):
    devices = mesh.devices.reshape(YH, YL, ZL, CORE, X, ZH)
    fine = Mesh(devices, AXES)
    prefix, sample = AXES[:4], AXES[4:]
    owner = P(prefix + sample)
    in_specs = (owner, P(prefix, sample), owner, owner, owner)
    return jax.shard_map(per_device, mesh=fine, in_specs=in_specs, out_specs=owner, check_vma=False)
```

```python
import functools
import math

import jax
import jax.numpy as jnp
from jax import lax
from jax.experimental import pallas as pl
from jax.experimental.pallas import tpu as pltpu
from jax.sharding import Mesh, PartitionSpec as P

F32 = jnp.float32
BF16 = jnp.bfloat16
LANES = 128
Y, ZL, CORE, X, ZH = 4, 4, 2, 4, 2
AXES = ("y", "zl", "core", "x", "zh")
WIDE = ("zl", "x", "zh")
SWAP = [(0, 1), (1, 0)]
BITS = 14.9
FRACTION = 32767.0
MASKED = -1e30
VMEM = pl.BlockSpec(memory_space=pltpu.VMEM)
HBM = pl.BlockSpec(memory_space=pltpu.HBM)
SMEM = pl.BlockSpec(memory_space=pltpu.SMEM)


def params(mib):
    return pltpu.CompilerParams(vmem_limit_bytes=mib * 2**20)


def lane_select(shape, columns):
    lane = lax.broadcasted_iota(jnp.int32, shape, 1)
    out = jnp.zeros(shape, F32)
    for i, column in enumerate(columns):
        out = jnp.where(lane == i, column, out)
    return out


def toward_zero(values):
    return values.astype(jnp.int32).astype(F32)


def code(values):
    peak = jnp.maximum(jnp.max(jnp.abs(values), axis=1, keepdims=True), 1e-30)
    power = toward_zero(jnp.log2(peak) + 129.0) - 128.0
    coded = jnp.round(values * jnp.exp2(BITS - power))
    return coded.astype(jnp.int32).astype(jnp.int16), power


def split_weight(weight):
    whole = toward_zero(weight * 0.5)
    return whole, (weight - 2.0 * whole) * (0.5 * FRACTION)


def join_weight(whole, part):
    return 2.0 * whole + part * (2.0 / FRACTION)


def spread_kernel(q_ref, out_ref, held_ref, rows_ref, sem, *, copies):
    copy = pltpu.make_async_copy(q_ref, held_ref, sem)
    copy.start()
    copy.wait()
    steps = q_ref.shape[1]
    tiles = q_ref.shape[2] // LANES
    for c in range(tiles):
        rows_ref[steps * c : steps * (c + 1), :] = held_ref[0, :, LANES * c : LANES * (c + 1)].astype(F32)
    rows = rows_ref[...].astype(BF16)
    for i in range(copies):
        out_ref[i] = rows


def spread(queries):
    count = queries.shape[1] * queries.shape[2] // LANES
    return pl.pallas_call(
        functools.partial(spread_kernel, copies=ZL),
        out_shape=jax.ShapeDtypeStruct((ZL, count, LANES), BF16),
        in_specs=[HBM],
        out_specs=VMEM,
        scratch_shapes=[
            pltpu.VMEM(queries.shape, BF16),
            pltpu.VMEM((count, LANES), F32),
            pltpu.SemaphoreType.DMA(()),
        ],
        compiler_params=params(16),
        name="spread",
    )(pltpu.with_memory_space_constraint(queries, pltpu.HBM))


def local_kernel(
    len_ref, q_ref, cache_ref, new_ref, numer_ref, stat_ref, kv_ref, new_pad, s_ref, sems, *, heads, chunk, factor
):
    rows = q_ref.shape[1]
    group = rows // heads
    total = cache_ref.shape[0]
    news = new_ref.shape[0]
    new_pad[...] = jnp.zeros_like(new_pad)
    pieces = sems.shape[0] - 1
    size = total // pieces
    copies = [
        pltpu.make_async_copy(cache_ref.at[pl.ds(i * size, size)], kv_ref.at[pl.ds(i * size, size)], sems.at[i])
        for i in range(pieces)
    ]
    copies.append(pltpu.make_async_copy(new_ref, new_pad.at[pl.ds(0, news)], sems.at[pieces]))
    for copy in copies:
        copy.start()
    q = q_ref[0]
    lane = lax.broadcasted_iota(jnp.int32, (rows, chunk), 1)
    row = lax.broadcasted_iota(jnp.int32, (rows, chunk), 0)
    own = (lane % heads) == (row // group)
    limit = jnp.where(own, lane, total)
    used = len_ref[0] * heads
    peak = None
    for j in range(total // chunk):
        if j * chunk % size == 0:
            copies[j * chunk // size].wait()
        s = lax.dot_general(
            q, kv_ref[j * chunk : (j + 1) * chunk, :LANES], (((1,), (1,)), ((), ())), preferred_element_type=F32
        )
        s = jnp.where(limit < used - j * chunk, s, MASKED)
        s_ref[:, j * chunk : (j + 1) * chunk] = s
        for i in range(chunk // LANES):
            part = s[:, i * LANES : (i + 1) * LANES]
            peak = part if peak is None else jnp.maximum(peak, part)
    copies[pieces].wait()
    s_new = lax.dot_general(q, new_pad[:, :LANES], (((1,), (1,)), ((), ())), preferred_element_type=F32)
    steps = news // heads
    lane = lane[:, :LANES]
    row = row[:, :LANES]
    valid = own[:, :LANES] & (lane // heads <= row % steps)
    s_new = jnp.where(valid, s_new, MASKED)
    peak = jnp.max(jnp.maximum(peak, s_new), axis=1, keepdims=True)
    p_new = jnp.exp2((s_new - peak) * factor)
    weight = p_new
    numer = jnp.dot(p_new.astype(BF16), new_pad[:, LANES:], preferred_element_type=F32)
    for j in range(total // chunk):
        p = jnp.exp2((s_ref[:, j * chunk : (j + 1) * chunk] - peak) * factor)
        for i in range(chunk // LANES):
            weight = weight + p[:, i * LANES : (i + 1) * LANES]
        numer = numer + jnp.dot(
            p.astype(BF16), kv_ref[j * chunk : (j + 1) * chunk, LANES:], preferred_element_type=F32
        )
    numer_ref[...] = numer
    scale = factor / math.log2(math.e)
    stat_ref[...] = lane_select((rows, LANES), (peak * scale, jnp.sum(weight, axis=1, keepdims=True)))


def local(lengths, rows, cache, new, heads, factor):
    count = rows.shape[1]
    pieces = 8
    return pl.pallas_call(
        functools.partial(local_kernel, heads=heads, chunk=512, factor=factor),
        out_shape=(jax.ShapeDtypeStruct((count, LANES), F32), jax.ShapeDtypeStruct((count, LANES), F32)),
        in_specs=[SMEM, VMEM, HBM, HBM],
        out_specs=(VMEM, VMEM),
        scratch_shapes=[
            pltpu.VMEM(cache.shape, BF16),
            pltpu.VMEM((LANES, 2 * LANES), BF16),
            pltpu.VMEM((count, cache.shape[0]), F32),
            pltpu.SemaphoreType.DMA((pieces + 1,)),
        ],
        compiler_params=params(24),
        name="local",
    )(lengths, rows, *(pltpu.with_memory_space_constraint(a, pltpu.HBM) for a in (cache, new)))


def document_kernel(*refs, groups, fetch, tile, chunk, factor):
    q_refs, kv = refs[:groups], list(refs[groups : groups + 2])
    out_refs = refs[groups + 2 : 2 * groups + 2]
    held = refs[2 * groups + 2 : 2 * groups + 4]
    rows = q_refs[0].shape[0]
    positions = kv[0].shape[0]
    copies = []
    if fetch:
        far_ref, (kv[1], sems) = kv[1], refs[2 * groups + 4 :]
        size = positions // sems.shape[0]
        for i in range(sems.shape[0]):
            at = pl.ds(i * size, size)
            copies.append(pltpu.make_async_copy(far_ref.at[at], kv[1].at[at], sems.at[i]))
            copies[i].start()
    pieces = positions // chunk
    tiles = rows // tile
    units = [(g, b, r) for g in range(groups) for b in range(2) for r in range(tiles)]
    scale = factor / math.log2(math.e)

    def scores(u, j):
        g, b, r = units[u]
        if u == tiles and j == 0:
            for copy in copies:
                copy.wait()
        s = lax.dot_general(
            q_refs[g][r * tile : (r + 1) * tile, :],
            kv[b][j * chunk : (j + 1) * chunk, :LANES],
            (((1,), (1,)), ((), ())),
            preferred_element_type=F32,
        )
        held[u % 2][:, j * chunk : (j + 1) * chunk] = s
        peak = s[:, :LANES]
        for i in range(1, chunk // LANES):
            peak = jnp.maximum(peak, s[:, i * LANES : (i + 1) * LANES])
        return peak

    running = None
    for j in range(pieces):
        part = scores(0, j)
        running = part if running is None else jnp.maximum(running, part)
    done = {}
    stats = []
    for u, (g, b, r) in enumerate(units):
        peak = jnp.max(running, axis=1, keepdims=True)
        running = total = numer = None
        for j in range(pieces):
            if u + 1 < len(units):
                part = scores(u + 1, j)
                running = part if running is None else jnp.maximum(running, part)
            p = jnp.exp2((held[u % 2][:, j * chunk : (j + 1) * chunk] - peak) * factor)
            for i in range(chunk // LANES):
                part = p[:, i * LANES : (i + 1) * LANES]
                total = part if total is None else total + part
            part = jnp.dot(
                p.astype(BF16), kv[b][j * chunk : (j + 1) * chunk, LANES:], preferred_element_type=F32
            )
            numer = part if numer is None else numer + part
        done[b, r] = (peak, jnp.sum(total, axis=1, keepdims=True), numer)
        if b == 1:
            (peak0, total0, numer0), (peak1, total1, numer1) = done[0, r], done[1, r]
            base = toward_zero(jnp.maximum(peak0, peak1) * (2.0 * scale))
            ground = base * (0.5 / scale)
            factor0 = jnp.exp2((peak0 - ground) * factor)
            factor1 = jnp.exp2((peak1 - ground) * factor)
            coded, power = code(numer0 * factor0 + numer1 * factor1)
            out_refs[g][r * tile : (r + 1) * tile, :] = coded
            weight = total0 * factor0 + total1 * factor1
            for i in range(tile // LANES):
                at = slice(i * LANES, (i + 1) * LANES)
                stats.append((base[at], weight[at], weight[at], power[at]))
            if len(stats) * LANES == rows:
                side = lane_select((LANES, LANES), [stat[j] for j in range(4) for stat in stats])
                whole, part = split_weight(side)
                lane = lax.broadcasted_iota(jnp.int32, (LANES, LANES), 1) // len(stats)
                side = jnp.where(lane == 1, whole, jnp.where(lane == 2, part, side))
                out_refs[g][rows : rows + LANES, :] = side.astype(jnp.int32).astype(jnp.int16)
                stats = []


def document(groups, kv0, kv1, factor, fetch=False):
    count = groups[0].shape[0]
    tile = 256
    out = jax.ShapeDtypeStruct((count + LANES, LANES), jnp.int16)
    scratch = [pltpu.VMEM((tile, kv0.shape[0]), F32)] * 2
    if fetch:
        kv1 = pltpu.with_memory_space_constraint(kv1, pltpu.HBM)
        scratch += [pltpu.VMEM(kv1.shape, BF16), pltpu.SemaphoreType.DMA((2,))]
    return pl.pallas_call(
        functools.partial(
            document_kernel, groups=len(groups), fetch=fetch, tile=tile, chunk=512, factor=factor
        ),
        out_shape=[out] * len(groups),
        in_specs=[VMEM] * (len(groups) + 1) + [HBM if fetch else VMEM],
        out_specs=[VMEM] * len(groups),
        scratch_shapes=scratch,
        compiler_params=params(40),
        name="document",
    )(*groups, kv0, kv1)


def merge_kernel(*refs):
    parts, out_ref = refs[:-1], refs[-1]
    blocks = 4
    owners = LANES // 16
    rows = parts[0].shape[0] - LANES
    lane = lax.broadcasted_iota(jnp.int32, (LANES, LANES), 1)

    def shifted(values, lanes):
        return pltpu.roll(values, lanes % LANES, 1)

    stats = [p[rows : rows + LANES, :].astype(jnp.int32).astype(F32) for p in parts]
    top = functools.reduce(jnp.maximum, stats)
    shrink = [jnp.exp(jnp.minimum(s - top, 0.0) * 0.5) for s in stats]
    weight = sum(f * join_weight(shifted(s, -blocks), shifted(s, -2 * blocks)) for f, s in zip(shrink, stats))
    whole, part = split_weight(weight)
    scales = [f * jnp.exp2(shifted(s, -3 * blocks) - BITS) for f, s in zip(shrink, stats)]
    side = jnp.where(lane < blocks, top, jnp.where(lane < 2 * blocks, shifted(whole, blocks), shifted(part, 2 * blocks)))
    for b in range(blocks):
        numer = None
        for p, scale in zip(parts, scales):
            term = p[b * LANES : (b + 1) * LANES, :].astype(jnp.int32).astype(F32) * scale[:, b : b + 1]
            numer = term if numer is None else numer + term
        coded, power = code(numer)
        tile = side if b == 0 else shifted(side, -b)
        tile = jnp.where(lane < 3 * blocks, tile, power)
        for s in range(owners):
            out_ref[b * owners + s, 0:16, :] = coded[16 * s : 16 * (s + 1), :]
            low, high = tile[16 * s : 16 * s + 8, :], shifted(tile[16 * s + 8 : 16 * s + 16, :], 16)
            packed = jnp.where(lane[:8] < 16, low, high)
            out_ref[b * owners + s, 16:24, :] = packed.astype(jnp.int32).astype(jnp.int16)


def merge(parts):
    return pl.pallas_call(
        merge_kernel,
        out_shape=jax.ShapeDtypeStruct((32, 24, LANES), jnp.int16),
        in_specs=[VMEM] * len(parts),
        out_specs=VMEM,
        compiler_params=params(32),
        name="merge",
    )(*parts)


def finish_kernel(got_ref, numer_ref, stat_ref, out_ref, rows_ref, *, heads):
    steps = out_ref.shape[1]
    def read(z, first, count):
        part = got_ref[z * heads : (z + 1) * heads, first : first + count, :]
        return part.astype(jnp.int32).astype(F32).reshape(-1, LANES)

    def unpack(packed):
        moved = pltpu.roll(packed, LANES - 16, 1)
        both = [part[8 * k : 8 * (k + 1)] for k in range(heads) for part in (packed, moved)]
        return jnp.concatenate(both, axis=0)

    tiles = [unpack(read(z, 16, 8)) for z in range(ZL)]
    peak = stat_ref[:, 0:1]
    tops = [t[:, 0:1] * 0.5 for t in tiles]
    top = functools.reduce(jnp.maximum, tops, peak)
    shrink = jnp.exp(peak - top)
    numer = numer_ref[...] * shrink
    weight = stat_ref[:, 1:2] * shrink
    for z, t in enumerate(tiles):
        shrink = jnp.exp(tops[z] - top)
        weight = weight + shrink * join_weight(t[:, 4:5], t[:, 8:9])
        numer = numer + read(z, 0, 16) * (shrink * jnp.exp2(t[:, 12:13] - BITS))
    rows_ref[...] = numer / weight
    for c in range(out_ref.shape[2] // LANES):
        out_ref[0, :, LANES * c : LANES * (c + 1)] = rows_ref[steps * c : steps * (c + 1), :].astype(BF16)


def finish(got, numer, stat, shape, heads):
    return pl.pallas_call(
        functools.partial(finish_kernel, heads=heads),
        out_shape=jax.ShapeDtypeStruct(shape, BF16),
        in_specs=[VMEM] * 3,
        out_specs=VMEM,
        scratch_shapes=[pltpu.VMEM(numer.shape, F32)],
        compiler_params=params(16),
        name="finish",
    )(got, numer, stat)


def per_device(queries, prefix_kv, suffix_kv, new_kv, lengths):
    positions, _, width = prefix_kv.shape
    head_dim = width // 2
    heads = suffix_kv.shape[2]
    factor = math.log2(math.e) / math.sqrt(head_dim)
    kv_own = prefix_kv.reshape(positions, width)
    kv_other = lax.ppermute(kv_own, "core", SWAP)
    spread_rows = spread(queries)
    gathered = lax.all_to_all(
        spread_rows.reshape(ZL * heads, -1, LANES), WIDE, split_axis=0, concat_axis=0, tiled=True
    ).reshape(-1, LANES)

    def exchange(array, bits):
        return lax.ppermute(array, "y", [(j, j ^ bits) for j in range(Y)])

    others = [exchange(gathered, bits) for bits in (1, 3, 2)]
    parts = document(others[:1], kv_other, kv_own, factor, fetch=True)
    parts, others = lax.optimization_barrier((parts, others))
    parts += document(others[1:], kv_own, kv_other, factor)
    parts = lax.optimization_barrier(parts)
    parts = [exchange(part, bits) for bits, part in zip((1, 3, 2), parts)]
    parts += document([gathered], kv_own, kv_other, factor)
    merged = merge(parts)
    merged, spread_rows = lax.optimization_barrier((merged, spread_rows))
    got = lax.all_to_all(merged, WIDE, split_axis=0, concat_axis=0, tiled=True)
    cache = suffix_kv.reshape(-1, width)
    numer, stat = local(lengths, spread_rows, cache, new_kv.reshape(-1, width), heads, factor)
    return finish(got, numer, stat, queries.shape, heads)


def solution(mesh):
    devices = mesh.devices.reshape(Y, ZL, CORE, X, ZH)
    fine = Mesh(devices, AXES)
    prefix, sample = AXES[:3], AXES[3:]
    owner = P(prefix + sample)
    in_specs = (owner, P(prefix, sample), owner, owner, owner)
    return jax.shard_map(per_device, mesh=fine, in_specs=in_specs, out_specs=owner, check_vma=False)
```
